512 devices in a mesh: island: 16 (over z_lo, core), shard: 32 (over z_hi, x, y).
Axes of the slice: x: 4, y: 4, z: 16 (z_hi: 2, z_lo: 8; z = z_hi * 8 + z_lo), core: 2. Of those that a mesh axis runs over, the one named last changes fastest.
Arguments:
- features: bfloat16 [16, 4096, 2304], P('island', 'shard'), may hold values from -6 to 6
- key_grads: bfloat16 [16, 4096, 1024], P('island', 'shard'), may hold values from -0.119628906 to 0.119628906
- key_weight: bfloat16 [16, 2304, 1024], P('island', 'shard'), may hold values from -0.125 to 0.125
- weight_first: float32 [16, 2304, 1024], P('island', 'shard'), may hold values from -3 to 3
- weight_second: float32 [16, 2304, 1024], P('island', 'shard'), may hold values from 0.1 to 4
- norm_gain: float32 [16, 2304], P('island'), may hold values from 0.5 to 1.5
- gain_first: float32 [16, 2304], P('island'), may hold values from -2 to 2
- gain_second: float32 [16, 2304], P('island'), may hold values from 0.05 to 2
- outer_params: float32 [4608, 1024], P('shard'), may hold values from -6 to 6
- island_params: bfloat16 [16, 4608, 1024], P('island', 'shard'), may hold values from -6 to 6
- outer_momentum: float32 [4608, 1024], P('shard', 'island'), may hold values from -3 to 3
Outputs:
- keys: bfloat16 [16, 4096, 1024], P('island', 'shard')
- new_weight: bfloat16 [16, 2304, 1024], P('island', 'shard')
- new_weight_first: float32 [16, 2304, 1024], P('island', 'shard')
- new_weight_second: float32 [16, 2304, 1024], P('island', 'shard')
- new_gain: float32 [16, 2304], P('island')
- new_gain_first: float32 [16, 2304], P('island')
- new_gain_second: float32 [16, 2304], P('island')
- new_outer: float32 [4608, 1024], P('shard')
- new_momentum: float32 [4608, 1024], P('shard', 'island')
The draws below stay inside these ranges and needn't reach their ends.
All inputs are finite; a program needn't handle non-finite values.
Results may differ from the reference program's by a relative error of at most 0.0037.
The reference program's roundings to bfloat16 on the way (of `normed`) count: a program that leaves them out, or rounds other values in their place, can miss the bound.
Values may be sent and summed in bfloat16 or wider, within the bound.
No kernel may reach another device: no remote copies, remote signals or barrier semaphores. Data moves between devices by JAX's collectives and lax.ppermute only.
A program may use at most 64 MiB of HBM per device.

```python
import math
import jax
import jax.numpy as jnp
from jax import lax

D = 4608
DW = 2304
KW = 1024
ROWS = 4096
ISLANDS = 16


def shard_levels(own_key, extent, shards, smallest, largest):
    level = 1.0
    for position, parts in shards:
        heights = jax.random.uniform(jax.random.fold_in(jax.random.fold_in(own_key, 6), position), (parts,), jnp.float32, smallest / len(shards), largest / len(shards))
        level = level * jnp.repeat(jnp.exp(heights), extent[position] // parts).reshape((-1,) + (1,) * (len(extent) - 1 - position))
    return level


def normal_values(own_key, extent, width, most, shards=(), kind=jnp.bfloat16):
    drawn = width * jax.random.normal(own_key, extent, jnp.float32)
    if shards:
        drawn = drawn * shard_levels(own_key, extent, shards, -0.22, 0.18)
    return jnp.clip(drawn, -most, most).astype(kind)


def setup_inputs(seed: int = 0) -> dict:
    key_of = jax.random.split(jax.random.key(seed), 12)
    return {
        "features": normal_values(key_of[0], (ISLANDS, ROWS, DW), 1.0, 6.0, ((0, 16), (1, 32))),
        "key_grads": normal_values(key_of[1], (ISLANDS, ROWS, KW), 0.02, 0.119628906, ((0, 16), (1, 32))),
        "key_weight": normal_values(key_of[2], (ISLANDS, DW, KW), DW ** -0.5, 0.125, ((0, 16), (1, 32))),
        "weight_first": normal_values(key_of[3], (ISLANDS, DW, KW), 0.5, 3.0, ((0, 16), (1, 32)), jnp.float32),
        "weight_second": jnp.clip(jnp.exp(math.log(4.0) - 3.6888794 * jax.random.uniform(key_of[4], (ISLANDS, DW, KW), jnp.float32) ** shard_levels(key_of[4], (ISLANDS, DW, KW), ((0, 16), (1, 32)), -0.2, 0.2)), 0.1, 4.0),
        "norm_gain": jnp.clip(1.0 + 0.1 * jax.random.normal(key_of[5], (ISLANDS, DW), jnp.float32), 0.5, 1.5),
        "gain_first": normal_values(key_of[6], (ISLANDS, DW), 0.3, 2.0, ((0, 16),), jnp.float32),
        "gain_second": jnp.clip(jnp.exp(math.log(2.0) - 3.6888794 * jax.random.uniform(key_of[7], (ISLANDS, DW), jnp.float32) ** shard_levels(key_of[7], (ISLANDS, DW), ((0, 16),), -0.2, 0.2)), 0.05, 2.0),
        "outer_params": normal_values(key_of[8], (D, KW), 1.0, 6.0, ((0, 32),), jnp.float32),
        "island_params": normal_values(key_of[9], (ISLANDS, D, KW), 1.0, 6.0, ((0, 16), (1, 32))),
        "outer_momentum": normal_values(key_of[10], (D, KW), 0.5, 3.0, ((0, 32), (1, 16)), jnp.float32),
    }


beta_first = 0.9
beta_second = 0.95
adam_floor = 1e-08
weight_decay = 0.1
rate_weight = 0.02
rate_gain = 0.01
momentum_keep = 0.9
rate_outer = 0.7
norm_epsilon = 1e-06

def adamw(param, grad, first, second, rate):
    first_new = beta_first * first + (1.0 - beta_first) * grad
    second_new = beta_second * second + (1.0 - beta_second) * grad * grad
    update = first_new / (jnp.sqrt(second_new) + adam_floor) + weight_decay * param
    return (param - rate * update, first_new, second_new)

def reference(features, key_grads, key_weight, weight_first, weight_second, norm_gain, gain_first, gain_second, outer_params, island_params, outer_momentum):
    keys_all, weight_all, wfirst_all, wsecond_all = ([], [], [], [])
    gain_all, gfirst_all, gsecond_all = ([], [], [])
    total = jnp.zeros(outer_params.shape, jnp.float32)
    for island in range(ISLANDS):
        rows = features[island].astype(jnp.float32)
        scaled = rows * lax.rsqrt(lax.optimization_barrier(jnp.mean(rows * rows, axis=1, keepdims=True)) + norm_epsilon)
        normed = (scaled * norm_gain[island]).astype(jnp.bfloat16)
        weight = key_weight[island]
        grads = key_grads[island]
        keys_all.append(jnp.dot(normed, weight, preferred_element_type=jnp.float32).astype(jnp.bfloat16))
        back = jnp.dot(grads, weight.T, preferred_element_type=jnp.float32)
        gain_grad = lax.optimization_barrier(jnp.sum(scaled * back, axis=0))
        weight_grad = jnp.dot(normed.T, grads, preferred_element_type=jnp.float32)
        new_w, new_wf, new_ws = adamw(weight.astype(jnp.float32), weight_grad, weight_first[island], weight_second[island], rate_weight)
        weight_all.append(new_w.astype(jnp.bfloat16))
        wfirst_all.append(new_wf)
        wsecond_all.append(new_ws)
        new_g, new_gf, new_gs = adamw(norm_gain[island], gain_grad, gain_first[island], gain_second[island], rate_gain)
        gain_all.append(new_g)
        gfirst_all.append(new_gf)
        gsecond_all.append(new_gs)
        total = total + (outer_params - island_params[island].astype(jnp.float32))
    drift = total / ISLANDS
    new_momentum = momentum_keep * outer_momentum + drift
    new_outer = outer_params - rate_outer * (drift + momentum_keep * new_momentum)
    return (jnp.stack(keys_all), jnp.stack(weight_all), jnp.stack(wfirst_all), jnp.stack(wsecond_all), jnp.stack(gain_all), jnp.stack(gfirst_all), jnp.stack(gsecond_all), new_outer, new_momentum)
```

```python
import functools

import jax
import jax.numpy as jnp
from jax import lax
from jax.experimental import pallas as pl
from jax.experimental.pallas import tpu as pltpu
from jax.sharding import Mesh, PartitionSpec as P

beta_first = 0.9
beta_second = 0.95
adam_floor = 1e-08
weight_decay = 0.1
rate_weight = 0.02
rate_gain = 0.01
momentum_keep = 0.9
rate_outer = 0.7
norm_epsilon = 1e-06

bf16 = jnp.bfloat16
f32 = jnp.float32

ZL, CORE, ZH, NX, NY = 8, 2, 2, 4, 4
ISLAND = ("zl", "core")
SHARD = ("zh", "x", "y")
VMEM = pl.BlockSpec(memory_space=pltpu.VMEM)
SMEM = pl.BlockSpec(memory_space=pltpu.SMEM)


def call(body, out_shape, n_in, *, scalars=0, flops=0, moved=1 << 20):
    return pl.pallas_call(
        body,
        out_shape=out_shape,
        in_specs=[SMEM] * scalars + [VMEM] * n_in,
        out_specs=jax.tree.map(lambda _: VMEM, out_shape),
        compiler_params=pltpu.CompilerParams(vmem_limit_bytes=40 << 20),
        cost_estimate=pl.CostEstimate(flops=flops, bytes_accessed=moved, transcendentals=0),
    )


def adamw(param, grad, first, second, rate):
    first_new = beta_first * first + (1.0 - beta_first) * grad
    second_new = beta_second * second + (1.0 - beta_second) * grad * grad
    update = first_new / (jnp.sqrt(second_new) + adam_floor) + weight_decay * param
    return (param - rate * update, first_new, second_new)


def diff_body(place, outer, island, out, own):
    rows = outer.shape[0] // 2
    zl, core = place[0], place[1]
    low = lax.broadcasted_iota(jnp.int32, (rows, 128), 1) < 64
    for pair in range(outer.shape[1] // 128):
        cols = slice(128 * pair, 128 * pair + 128)
        delta = outer[:, cols] - island[:, cols].astype(f32)
        top, bottom = delta[:rows], delta[rows:]
        out[2 * pair] = jnp.where(low, top, pltpu.roll(bottom, 64, 1)).astype(bf16)
        out[2 * pair + 1] = jnp.where(low, pltpu.roll(top, 64, 1), bottom).astype(bf16)
    mine = outer[:, pl.ds(pl.multiple_of(zl * 128, 128), 128)]
    top, bottom = mine[:rows], mine[rows:]
    own[...] = jnp.where(
        core == 0,
        jnp.where(low, top, pltpu.roll(bottom, 64, 1)),
        jnp.where(low, pltpu.roll(top, 64, 1), bottom),
    )


def norm_body(features, grads, gain, out):
    rows = features[...].astype(f32)
    scaled = rows * lax.rsqrt(jnp.mean(rows * rows, axis=1, keepdims=True) + norm_epsilon)
    turned = jnp.transpose(scaled * gain[...])
    width = turned.shape[0] // (ZH * NX * NY)
    turned_grads = jnp.transpose(grads[...].astype(f32)).astype(bf16)
    for y in range(NY):
        parts = []
        for x in range(NX):
            for zh in range(ZH):
                at = ((zh * NX + x) * NY + y) * width
                parts.append(turned[at : at + width])
        block = jnp.concatenate(parts, axis=0).astype(bf16)
        out[y, : block.shape[0], :] = block
        out[y, block.shape[0] :, :] = turned_grads


def dw_body(got, out):
    part = out.shape[1]
    wide = NX * part
    grads = jnp.concatenate([got[s, wide:, :] for s in range(NY)], axis=1)
    for x in range(NX):
        rows = slice(x * part, (x + 1) * part)
        normed = jnp.concatenate([got[s, rows, :] for s in range(NY)], axis=1)
        out[x] = lax.dot_general(
            normed, grads, (((1,), (1,)), ((), ())), preferred_element_type=f32
        ).astype(bf16)


def keys_body(got, weight, out):
    wide = weight.shape[0]
    for s in range(NY):
        out[s] = lax.dot_general(
            got[s, :wide, :], weight[...], (((0,), (0,)), ((), ())), preferred_element_type=f32
        ).astype(bf16)


def dwsum_body(zh_ref, got, weight, gain, own, gain_own, send):
    half = own.shape[0]
    width = own.shape[1]
    low = zh_ref[0] == 0
    total = got[0].astype(f32)
    for s in range(1, NX):
        total = total + got[s].astype(f32)
    dots = jnp.sum(total * weight[...].astype(f32), axis=1, keepdims=True) / gain[...]
    own[...] = jnp.where(low, total[:half], total[half:])
    send[:, :width] = jnp.where(low, total[half:], total[:half]).astype(bf16)
    lane = lax.broadcasted_iota(jnp.int32, (half, 128), 1)
    first, second = dots[:half], dots[half:]
    gain_own[...] = jnp.where(lane == 0, first, second)
    first_hi, second_hi = first.astype(bf16).astype(f32), second.astype(bf16).astype(f32)
    packed = jnp.where(
        lane == 0,
        first_hi,
        jnp.where(lane == 1, second_hi, jnp.where(lane == 2, first - first_hi, second - second_hi)),
    )
    send[:, width:] = packed.astype(bf16)


def local(
    features,
    key_grads,
    key_weight,
    weight_first,
    weight_second,
    norm_gain,
    gain_first,
    gain_second,
    outer_params,
    island_params,
    outer_momentum,
):
    tokens, wide = features.shape[1:]
    width = key_weight.shape[2]
    part = wide // (ZH * NX * NY)
    group = wide // NY
    n_island = ZL * CORE
    rows = outer_params.shape[0]
    zh, x, y = (lax.axis_index(a) for a in SHARD)
    weight = key_weight[0]

    pair_weight = lax.all_gather(weight, "zh", axis=0, tiled=True)
    group_weight = lax.all_gather(pair_weight, "x", axis=0, tiled=True)

    place = jnp.stack([lax.axis_index("zl"), lax.axis_index("core")]).astype(jnp.int32)
    sent, own_outer = call(
        diff_body,
        (
            jax.ShapeDtypeStruct((n_island, rows // 2, 128), bf16),
            jax.ShapeDtypeStruct((rows // 2, 128), f32),
        ),
        2,
        scalars=1,
    )(place, outer_params, island_params[0])
    sent = lax.all_to_all(sent, ISLAND, 0, 0, tiled=True)
    drift = jnp.sum(sent.astype(f32), axis=0) / n_island
    moment = jnp.concatenate([outer_momentum[: rows // 2], outer_momentum[rows // 2 :]], axis=1)
    moment = momentum_keep * moment + drift
    new_momentum = jnp.concatenate([moment[:, :64], moment[:, 64:]], axis=0)
    step = own_outer - rate_outer * (drift + momentum_keep * moment)
    step = lax.all_to_all(
        jnp.broadcast_to(step.astype(bf16)[None], (n_island,) + step.shape), ISLAND, 0, 0, tiled=True
    )
    step = step.reshape(n_island, rows // 2, 2, 64).transpose(2, 1, 0, 3).reshape(rows, width)
    new_outer = step.astype(f32)

    got = call(norm_body, jax.ShapeDtypeStruct((NY, group + width, tokens), bf16), 3)(
        features[0], key_grads[0], norm_gain
    )
    got = lax.all_to_all(got, "y", 0, 0, tiled=True)
    partial = call(
        dw_body, jax.ShapeDtypeStruct((NX, ZH * part, width), bf16), 1, flops=2 * group * width * tokens * NY
    )(got)
    partial = lax.all_to_all(partial, "x", 0, 0, tiled=True)
    gain_pair = lax.dynamic_index_in_dim(
        norm_gain.reshape(ZH, NX * NY, part), x * NY + y, 1, keepdims=False
    )
    own, gain_own, send = call(
        dwsum_body,
        (
            jax.ShapeDtypeStruct((part, width), f32),
            jax.ShapeDtypeStruct((part, 128), f32),
            jax.ShapeDtypeStruct((part, width + 128), bf16),
        ),
        3,
        scalars=1,
    )(zh.astype(jnp.int32)[None], partial, pair_weight, gain_pair.reshape(ZH * part, 1))
    both = lax.all_gather(send, "zh", axis=0, tiled=False)
    other = lax.dynamic_index_in_dim(both, 1 - zh, 0, keepdims=False).astype(f32)
    weight_grad = own + other[:, :width]
    new_w, new_wf, new_ws = adamw(
        weight.astype(f32), weight_grad, weight_first[0], weight_second[0], rate_weight
    )

    keys = call(
        keys_body,
        jax.ShapeDtypeStruct((NY, tokens, width), bf16),
        2,
        flops=2 * group * width * tokens * NY,
    )(got, group_weight)
    keys = lax.all_to_all(keys, "y", 0, 0, tiled=True)
    keys = jnp.sum(keys.astype(f32), axis=0).astype(bf16)

    gain_sum = gain_own[:, :2] + (other[:, width : width + 2] + other[:, width + 2 : width + 4])
    tile = jnp.pad(gain_sum.T, ((0, 8 - ZH), (0, 128 - part)))
    tiles = lax.all_to_all(
        jnp.broadcast_to(tile[None], (NX * NY,) + tile.shape), ("x", "y"), 0, 0, tiled=True
    )
    gain_grad = tiles[:, :ZH, :part].transpose(1, 0, 2).reshape(1, wide)
    new_g, new_gf, new_gs = adamw(norm_gain, gain_grad, gain_first, gain_second, rate_gain)
    return (
        keys[None],
        new_w.astype(bf16)[None],
        new_wf[None],
        new_ws[None],
        new_g,
        new_gf,
        new_gs,
        new_outer,
        new_momentum,
    )


def solution(mesh):
    grid = Mesh(mesh.devices.reshape(ZL, CORE, ZH, NX, NY), ISLAND + SHARD)
    block = P(ISLAND, SHARD, None)
    vector = P(ISLAND, None)
    fragment = P(SHARD, None)
    momentum = P(SHARD, ISLAND)
    return jax.shard_map(
        local,
        mesh=grid,
        in_specs=(block,) * 5 + (vector,) * 3 + (fragment, block, momentum),
        out_specs=(block,) * 4 + (vector,) * 3 + (fragment, momentum),
        check_vma=False,
    )
```

```python
import functools

import jax
import jax.numpy as jnp
from jax import lax
from jax.experimental import pallas as pl
from jax.experimental.pallas import tpu as pltpu
from jax.sharding import Mesh, PartitionSpec as P

beta_first = 0.9
beta_second = 0.95
adam_floor = 1e-08
weight_decay = 0.1
rate_weight = 0.02
rate_gain = 0.01
momentum_keep = 0.9
rate_outer = 0.7
norm_epsilon = 1e-06

bf16 = jnp.bfloat16
f32 = jnp.float32

ZL, CORE, ZH, NX, NY = 8, 2, 2, 4, 4
ISLAND = ("zl", "core")
SHARD = ("zh", "x", "y")
VMEM = pl.BlockSpec(memory_space=pltpu.VMEM)
ANY = pl.BlockSpec(memory_space=pl.ANY)
SMEM = pl.BlockSpec(memory_space=pltpu.SMEM)


def call(body, out_shape, n_in, *, scalars=0, after=0, flops=0, moved=1 << 20):
    return pl.pallas_call(
        body,
        out_shape=out_shape,
        in_specs=[SMEM] * scalars + [ANY] * after + [VMEM] * n_in,
        out_specs=jax.tree.map(lambda _: VMEM, out_shape),
        compiler_params=pltpu.CompilerParams(vmem_limit_bytes=40 << 20),
        cost_estimate=pl.CostEstimate(flops=flops, bytes_accessed=moved, transcendentals=0),
    )


def adamw(param, grad, first, second, rate):
    first_new = beta_first * first + (1.0 - beta_first) * grad
    second_new = beta_second * second + (1.0 - beta_second) * grad * grad
    update = first_new / (jnp.sqrt(second_new) + adam_floor) + weight_decay * param
    return (param - rate * update, first_new, second_new)


def pack(tile, low):
    rows = tile.shape[0] // 2
    top, bottom = tile[:rows], tile[rows:]
    return (
        jnp.where(low, top, pltpu.roll(bottom, 64, 1)),
        jnp.where(low, pltpu.roll(top, 64, 1), bottom),
    )


def low_lanes(rows):
    return lax.broadcasted_iota(jnp.int32, (rows, 128), 1) < 64


def diff_body(core_ref, outer, island, mine, theirs, outer_mine):
    low = low_lanes(mine.shape[1])
    first = core_ref[0] == 0
    for pair in range(mine.shape[0]):
        cols = slice(128 * pair, 128 * pair + 128)
        whole = outer[:, cols]
        even, odd = pack(whole - island[:, cols].astype(f32), low)
        mine[pair] = jnp.where(first, even, odd)
        theirs[pair] = jnp.where(first, odd, even)
        even, odd = pack(whole, low)
        outer_mine[pair] = jnp.where(first, even, odd)


def halves_body(zh_ref, weight, weight_got, pair_weight):
    own, other = weight[...].astype(f32), weight_got[...].astype(f32)
    lower = zh_ref[0] == 0
    pair_weight[...] = jnp.concatenate(
        [jnp.where(lower, own, other), jnp.where(lower, other, own)], axis=0
    ).astype(bf16)


def norm_body(features, grads, gain, out):
    rows = features[...].astype(f32)
    scaled = rows * lax.rsqrt(jnp.mean(rows * rows, axis=1, keepdims=True) + norm_epsilon)
    turned = jnp.transpose(scaled * gain[...])
    width = turned.shape[0] // (ZH * NX * NY)
    turned_grads = jnp.transpose(grads[...].astype(f32)).astype(bf16)
    for y in range(NY):
        parts = []
        for x in range(NX):
            for zh in range(ZH):
                at = ((zh * NX + x) * NY + y) * width
                parts.append(turned[at : at + width])
        block = jnp.concatenate(parts, axis=0).astype(bf16)
        out[y, : block.shape[0], :] = block
        out[y, block.shape[0] :, :] = turned_grads


def dw_body(zl_ref, after, got, mine, theirs, moment, out, step, packed):
    del after
    part = out.shape[1]
    wide = NX * part
    grads = jnp.concatenate([got[s, wide:, :] for s in range(NY)], axis=1)
    for x in range(NX):
        rows = slice(x * part, (x + 1) * part)
        normed = jnp.concatenate([got[s, rows, :] for s in range(NY)], axis=1)
        out[x] = lax.dot_general(
            normed, grads, (((1,), (1,)), ((), ())), preferred_element_type=f32
        ).astype(bf16)
    half = packed.shape[0]
    packed[...] = jnp.concatenate([moment[:half], moment[half:]], axis=1)
    own = momentum_keep * momentum_keep * packed[...]
    for pair in range(step.shape[0]):
        drift = (mine[pair] + theirs[pair]) * ((1.0 + momentum_keep) / (ZL * CORE))
        step[pair] = jnp.where(zl_ref[0] == pair, drift + own, drift).astype(bf16)


def dwsum_body(
    zh_ref, got, weight, own, gain_own, send
):
    half = own.shape[0]
    width = own.shape[1]
    low = zh_ref[0] == 0
    total = got[0].astype(f32)
    for s in range(1, NX):
        total = total + got[s].astype(f32)
    dots = jnp.sum(total * weight[...].astype(f32), axis=1, keepdims=True)
    own[...] = jnp.where(low, total[:half], total[half:])
    send[:, :width] = jnp.where(low, total[half:], total[:half]).astype(bf16)
    lane = lax.broadcasted_iota(jnp.int32, (half, 128), 1)
    first, second = dots[:half], dots[half:]
    first_hi, second_hi = first.astype(bf16).astype(f32), second.astype(bf16).astype(f32)
    first_lo = (first - first_hi).astype(bf16).astype(f32)
    second_lo = (second - second_hi).astype(bf16).astype(f32)
    packed = jnp.where(
        lane == 0,
        first_hi,
        jnp.where(lane == 1, second_hi, jnp.where(lane == 2, first_lo, second_lo)),
    )
    gain_own[...] = packed
    send[:, width:] = packed.astype(bf16)


def keys_body(x_ref, done, got, same, before, after, across, step, step_got, out, step_out):
    del done
    part = same.shape[0]
    for s in range(NY):
        total = None
        for by, weight in ((0, same), (NX - 1, before), (1, after), (2, across)):
            source = lax.rem(x_ref[0] + by, NX)
            rows = got[s, pl.ds(pl.multiple_of(source * part, part), part), :]
            term = lax.dot_general(
                rows, weight[...], (((0,), (0,)), ((), ())), preferred_element_type=f32
            )
            total = term if total is None else total + term
        out[s] = total.astype(bf16)
    step_out[...] = (step[...].astype(f32) + step_got[...].astype(f32)).astype(bf16)


def update_body(
    zl_ref,
    own,
    got,
    weight,
    first,
    second,
    gain_own,
    step,
    step_one,
    step_two,
    step_three,
    outer_mine,
    packed,
    keys_got,
    new_w,
    new_wf,
    new_ws,
    tiles,
    outer_out,
    moment_out,
    keys,
):
    width = own.shape[1]
    grad = own[...] + got[:, :width].astype(f32)
    w, wf, ws = adamw(weight[...].astype(f32), grad, first[...], second[...], rate_weight)
    new_w[...] = w.astype(bf16)
    new_wf[...] = wf
    new_ws[...] = ws
    mine, theirs = gain_own[...], got[:, width:].astype(f32)
    total = (mine + pltpu.roll(mine, 126, 1)) + (theirs + pltpu.roll(theirs, 126, 1))
    total = jnp.concatenate([total, jnp.zeros((128 - total.shape[0], 128), f32)], axis=0)
    total = jnp.transpose(total)[:8]
    for at in range(tiles.shape[0]):
        tiles[at] = total
    half = packed.shape[0]
    mine = jnp.zeros((half, 128), f32)
    for pair in range(step.shape[0]):
        both = (step[pair].astype(f32) + step_one[pair].astype(f32)) + (
            step_two[pair].astype(f32) + step_three[pair].astype(f32)
        )
        outer_out[pair] = outer_mine[pair] - rate_outer * both
        mine = jnp.where(zl_ref[0] == pair, both, mine)
    moment = packed[...]
    drift = (mine - momentum_keep * momentum_keep * moment) * (1.0 / (1.0 + momentum_keep))
    new = momentum_keep * moment + drift
    moment_out[:half] = new[:, :64]
    moment_out[half:] = new[:, 64:]
    sums = keys_got[0].astype(f32)
    for y in range(1, NY):
        sums = sums + keys_got[y].astype(f32)
    keys[...] = sums.astype(bf16)


def join_body(core_ref, mine, got, out):
    rows = mine.shape[1]
    low = low_lanes(rows)
    first = core_ref[0] == 0
    for pair in range(mine.shape[0]):
        even = jnp.where(first, mine[pair], got[pair])
        odd = jnp.where(first, got[pair], mine[pair])
        cols = slice(128 * pair, 128 * pair + 128)
        out[:rows, cols] = jnp.where(low, even, pltpu.roll(odd, 64, 1))
        out[rows:, cols] = jnp.where(low, pltpu.roll(even, 64, 1), odd)


def swap(value, axis):
    return lax.ppermute(value, axis, [(0, 1), (1, 0)])


def shift(value, axis, by, size=4):
    return lax.ppermute(value, axis, [(i, (i + by) % size) for i in range(size)])


def ring4(value, axis):
    return value, shift(value, axis, 1), shift(value, axis, -1), shift(value, axis, 2)


def partner(value, by):
    return lax.ppermute(value, "zl", [(i, i ^ by) for i in range(ZL)])


def local(
    features,
    key_grads,
    key_weight,
    weight_first,
    weight_second,
    norm_gain,
    gain_first,
    gain_second,
    outer_params,
    island_params,
    outer_momentum,
):
    tokens, wide = features.shape[1:]
    width = key_weight.shape[2]
    part = wide // (ZH * NX * NY)
    group = wide // NY
    rows = outer_params.shape[0]
    zl, core = (lax.axis_index(a).astype(jnp.int32) for a in ISLAND)
    zh, x, y = (lax.axis_index(a).astype(jnp.int32) for a in SHARD)
    weight = key_weight[0]
    shape = jax.ShapeDtypeStruct
    half = shape((width // 128, rows // 2, 128), f32)
    half_short = shape(half.shape, bf16)

    sent = call(norm_body, shape((NY, group + width, tokens), bf16), 3)(
        features[0], key_grads[0], norm_gain
    )
    got = lax.all_to_all(sent, "y", 0, 0, tiled=True)
    pair_weight = call(halves_body, shape((ZH * part, width), bf16), 2, scalars=1)(
        zh[None], weight, swap(weight, "zh")
    )
    mine, theirs, outer_mine = call(diff_body, (half, half, half), 2, scalars=1)(
        core[None], outer_params, island_params[0]
    )
    partial, step, packed = call(
        dw_body,
        (shape((NX, ZH * part, width), bf16), half_short, shape(half.shape[1:], f32)),
        4,
        scalars=1,
        after=1,
        flops=2 * group * width * tokens * NY,
    )(zl[None], pair_weight, got, mine, swap(theirs, "core"), outer_momentum)
    partial = lax.all_to_all(partial, "x", 0, 0, tiled=True)
    group_weight = ring4(pair_weight, "x")

    own, gain_own, send = call(
        dwsum_body,
        (shape((part, width), f32), shape((part, 128), f32), shape((part, width + 128), bf16)),
        2,
        scalars=1,
    )(zh[None], partial, pair_weight)
    grad_got = swap(send, "zh")
    keys, step = call(
        keys_body,
        (shape((NY, tokens, width), bf16), half_short),
        7,
        scalars=1,
        after=1,
        flops=2 * group * width * tokens * NY,
    )(x[None], own, got, *group_weight, step, partner(step, 4))
    keys_got = lax.all_to_all(keys, "y", 0, 0, tiled=True)

    moments = shape((part, width), f32)
    new_w, new_wf, new_ws, tiles, outer_half, new_momentum, keys = call(
        update_body,
        (
            shape((part, width), bf16),
            moments,
            moments,
            shape((NX * NY, 8, 128), f32),
            half,
            shape(outer_momentum.shape, f32),
            shape((tokens, width), bf16),
        ),
        13,
        scalars=1,
    )(
        zl[None],
        own,
        grad_got,
        weight,
        weight_first[0],
        weight_second[0],
        gain_own,
        step,
        partner(step, 1),
        partner(step, 2),
        partner(step, 3),
        outer_mine,
        packed,
        keys_got,
    )
    tiles = lax.all_to_all(tiles, ("x", "y"), 0, 0, tiled=True)
    new_outer = call(join_body, shape(outer_params.shape, f32), 2, scalars=1)(
        core[None], outer_half, swap(outer_half, "core")
    )
    gain_grad = tiles[:, :ZH, :part].transpose(1, 0, 2).reshape(1, wide) / norm_gain
    new_g, new_gf, new_gs = adamw(norm_gain, gain_grad, gain_first, gain_second, rate_gain)
    return (
        keys[None],
        new_w[None],
        new_wf[None],
        new_ws[None],
        new_g,
        new_gf,
        new_gs,
        new_outer,
        new_momentum,
    )


def solution(mesh):
    grid = Mesh(mesh.devices.reshape(ZL, CORE, ZH, NX, NY), ISLAND + SHARD)
    block = P(ISLAND, SHARD, None)
    vector = P(ISLAND, None)
    fragment = P(SHARD, None)
    momentum = P(SHARD, ISLAND)
    return jax.shard_map(
        local,
        mesh=grid,
        in_specs=(block,) * 5 + (vector,) * 3 + (fragment, block, momentum),
        out_specs=(block,) * 4 + (vector,) * 3 + (fragment, momentum),
        check_vma=False,
    )
```

```python
import functools

import jax
import jax.numpy as jnp
from jax import lax
from jax.experimental import pallas as pl
from jax.experimental.pallas import tpu as pltpu
from jax.sharding import Mesh, PartitionSpec as P

beta_first = 0.9
beta_second = 0.95
adam_floor = 1e-08
weight_decay = 0.1
rate_weight = 0.02
rate_gain = 0.01
momentum_keep = 0.9
rate_outer = 0.7
norm_epsilon = 1e-06

bf16 = jnp.bfloat16
f32 = jnp.float32

ZL, CORE, ZH, NX, NY = 8, 2, 2, 4, 4
ISLAND = ("zl", "core")
SHARD = ("zh", "x", "y")
VMEM = pl.BlockSpec(memory_space=pltpu.VMEM)
ANY = pl.BlockSpec(memory_space=pl.ANY)
SMEM = pl.BlockSpec(memory_space=pltpu.SMEM)


def call(body, out_shape, n_in, *, scalars=0, after=0, flops=0, moved=1 << 20):
    return pl.pallas_call(
        body,
        out_shape=out_shape,
        in_specs=[SMEM] * scalars + [ANY] * after + [VMEM] * n_in,
        out_specs=jax.tree.map(lambda _: VMEM, out_shape),
        compiler_params=pltpu.CompilerParams(vmem_limit_bytes=40 << 20),
        cost_estimate=pl.CostEstimate(flops=flops, bytes_accessed=moved, transcendentals=0),
    )


def adamw(param, grad, first, second, rate):
    first_new = beta_first * first + (1.0 - beta_first) * grad
    second_new = beta_second * second + (1.0 - beta_second) * grad * grad
    update = first_new / (jnp.sqrt(second_new) + adam_floor) + weight_decay * param
    return (param - rate * update, first_new, second_new)


def pack(tile, low):
    rows = tile.shape[0] // 2
    top, bottom = tile[:rows], tile[rows:]
    return (
        jnp.where(low, top, pltpu.roll(bottom, 64, 1)),
        jnp.where(low, pltpu.roll(top, 64, 1), bottom),
    )


def low_lanes(rows):
    return lax.broadcasted_iota(jnp.int32, (rows, 128), 1) < 64


def diff_body(core_ref, outer, island, mine, theirs, outer_mine):
    low = low_lanes(mine.shape[1])
    first = core_ref[0] == 0
    for pair in range(mine.shape[0]):
        cols = slice(128 * pair, 128 * pair + 128)
        whole = outer[:, cols]
        even, odd = pack(whole - island[:, cols].astype(f32), low)
        mine[pair] = jnp.where(first, even, odd)
        theirs[pair] = jnp.where(first, odd, even)
        even, odd = pack(whole, low)
        outer_mine[pair] = jnp.where(first, even, odd)


def halves_body(zh_ref, weight, weight_got, pair_weight):
    own, other = weight[...].astype(f32), weight_got[...].astype(f32)
    lower = zh_ref[0] == 0
    pair_weight[...] = jnp.concatenate(
        [jnp.where(lower, own, other), jnp.where(lower, other, own)], axis=0
    ).astype(bf16)


def norm_body(features, grads, gain, out):
    rows = features[...].astype(f32)
    scaled = rows * lax.rsqrt(jnp.mean(rows * rows, axis=1, keepdims=True) + norm_epsilon)
    turned = jnp.transpose(scaled * gain[...])
    width = turned.shape[0] // (ZH * NX * NY)
    turned_grads = jnp.transpose(grads[...].astype(f32)).astype(bf16)
    for y in range(NY):
        parts = []
        for x in range(NX):
            for zh in range(ZH):
                at = ((zh * NX + x) * NY + y) * width
                parts.append(turned[at : at + width])
        block = jnp.concatenate(parts, axis=0).astype(bf16)
        out[y, : block.shape[0], :] = block
        out[y, block.shape[0] :, :] = turned_grads


def dw_body(zl_ref, got, mine, theirs, moment, out, step, packed):
    part = out.shape[1]
    wide = NX * part
    grads = jnp.concatenate([got[s, wide:, :] for s in range(NY)], axis=1)
    for x in range(NX):
        rows = slice(x * part, (x + 1) * part)
        normed = jnp.concatenate([got[s, rows, :] for s in range(NY)], axis=1)
        out[x] = lax.dot_general(
            normed, grads, (((1,), (1,)), ((), ())), preferred_element_type=f32
        ).astype(bf16)
    half = packed.shape[0]
    packed[...] = jnp.concatenate([moment[:half], moment[half:]], axis=1)
    own = momentum_keep * momentum_keep * packed[...]
    for pair in range(step.shape[0]):
        drift = (mine[pair] + theirs[pair]) * ((1.0 + momentum_keep) / (ZL * CORE))
        step[pair] = jnp.where(zl_ref[0] == pair, drift + own, drift).astype(bf16)


def dwsum_body(zh_ref, got, weight, step, step_got, own, gain_own, send, step_out):
    half = own.shape[0]
    width = own.shape[1]
    low = zh_ref[0] == 0
    total = got[0].astype(f32)
    for s in range(1, NX):
        total = total + got[s].astype(f32)
    dots = jnp.sum(total * weight[...].astype(f32), axis=1, keepdims=True)
    own[...] = jnp.where(low, total[:half], total[half:])
    send[:, :width] = jnp.where(low, total[half:], total[:half]).astype(bf16)
    lane = lax.broadcasted_iota(jnp.int32, (half, 128), 1)
    first, second = dots[:half], dots[half:]
    first_hi, second_hi = first.astype(bf16).astype(f32), second.astype(bf16).astype(f32)
    first_lo = (first - first_hi).astype(bf16).astype(f32)
    second_lo = (second - second_hi).astype(bf16).astype(f32)
    packed = jnp.where(
        lane == 0,
        first_hi,
        jnp.where(lane == 1, second_hi, jnp.where(lane == 2, first_lo, second_lo)),
    )
    gain_own[...] = packed
    send[:, width:] = packed.astype(bf16)
    step_out[...] = (step[...].astype(f32) + step_got[...].astype(f32)).astype(bf16)


def keys_body(
    x_ref, y_ref, done, got, same, before, after, across, step, step_got, own, up, down, over, step_out
):
    del done
    part = same.shape[0]
    for to, out in ((0, own), (1, up), (NY - 1, down), (2, over)):
        s = lax.rem(y_ref[0] + to, NY)
        total = None
        for by, weight in ((0, same), (NX - 1, before), (1, after), (2, across)):
            source = lax.rem(x_ref[0] + by, NX)
            rows = got[s, pl.ds(pl.multiple_of(source * part, part), part), :]
            term = lax.dot_general(
                rows, weight[...], (((0,), (0,)), ((), ())), preferred_element_type=f32
            )
            total = term if total is None else total + term
        out[...] = total.astype(out.dtype)
    step_out[...] = step[...].astype(f32) + step_got[...].astype(f32)


def update_body(after, own, got, weight, first, second, gain_own, new_w, new_wf, new_ws, tiles):
    del after
    width = own.shape[1]
    grad = own[...] + got[:, :width].astype(f32)
    w, wf, ws = adamw(weight[...].astype(f32), grad, first[...], second[...], rate_weight)
    new_w[...] = w.astype(bf16)
    new_wf[...] = wf
    new_ws[...] = ws
    mine, theirs = gain_own[...], got[:, width:].astype(f32)
    total = (mine + pltpu.roll(mine, 126, 1)) + (theirs + pltpu.roll(theirs, 126, 1))
    total = jnp.concatenate([total, jnp.zeros((128 - total.shape[0], 128), f32)], axis=0)
    total = jnp.transpose(total)[:8]
    for at in range(tiles.shape[0]):
        tiles[at] = total


def step_body(zl_ref, step, step_got, outer_mine, packed, outer_out, moment_out):
    half = packed.shape[0]
    mine = jnp.zeros((half, 128), f32)
    for pair in range(outer_mine.shape[0]):
        both = step[pair] + step_got[pair]
        outer_out[pair] = outer_mine[pair] - rate_outer * both
        mine = jnp.where(zl_ref[0] == pair, both, mine)
    moment = packed[...]
    drift = (mine - momentum_keep * momentum_keep * moment) * (1.0 / (1.0 + momentum_keep))
    new = momentum_keep * moment + drift
    moment_out[:half] = new[:, :64]
    moment_out[half:] = new[:, 64:]


def sum_body(own, before, after, across, out):
    out[...] = (
        (own[...] + before[...].astype(f32)) + (after[...].astype(f32) + across[...].astype(f32))
    ).astype(bf16)


def join_body(core_ref, mine, got, out):
    rows = mine.shape[1]
    low = low_lanes(rows)
    first = core_ref[0] == 0
    for pair in range(mine.shape[0]):
        even = jnp.where(first, mine[pair], got[pair])
        odd = jnp.where(first, got[pair], mine[pair])
        cols = slice(128 * pair, 128 * pair + 128)
        out[:rows, cols] = jnp.where(low, even, pltpu.roll(odd, 64, 1))
        out[rows:, cols] = jnp.where(low, pltpu.roll(even, 64, 1), odd)


def swap(value, axis):
    return lax.ppermute(value, axis, [(0, 1), (1, 0)])


def shift(value, axis, by, size=4):
    return lax.ppermute(value, axis, [(i, (i + by) % size) for i in range(size)])


def ring4(value, axis):
    return value, shift(value, axis, 1), shift(value, axis, -1), shift(value, axis, 2)


def partner(value, by):
    return lax.ppermute(value, "zl", [(i, i ^ by) for i in range(ZL)])


def local(
    features,
    key_grads,
    key_weight,
    weight_first,
    weight_second,
    norm_gain,
    gain_first,
    gain_second,
    outer_params,
    island_params,
    outer_momentum,
):
    tokens, wide = features.shape[1:]
    width = key_weight.shape[2]
    part = wide // (ZH * NX * NY)
    group = wide // NY
    rows = outer_params.shape[0]
    zl, core = (lax.axis_index(a).astype(jnp.int32) for a in ISLAND)
    zh, x, y = (lax.axis_index(a).astype(jnp.int32) for a in SHARD)
    weight = key_weight[0]
    shape = jax.ShapeDtypeStruct
    half = shape((width // 128, rows // 2, 128), f32)
    half_short = shape(half.shape, bf16)

    sent = call(norm_body, shape((NY, group + width, tokens), bf16), 3)(
        features[0], key_grads[0], norm_gain
    )
    got = lax.all_to_all(sent, "y", 0, 0, tiled=True)
    pair_weight = call(
        halves_body, shape((ZH * part, width), bf16), 2, scalars=1, flops=int(1.3e10)
    )(
        zh[None], weight, swap(weight, "zh")
    )
    mine, theirs, outer_mine = call(diff_body, (half, half, half), 2, scalars=1)(
        core[None], outer_params, island_params[0]
    )
    partial, step, packed = call(
        dw_body,
        (shape((NX, ZH * part, width), bf16), half_short, shape(half.shape[1:], f32)),
        4,
        scalars=1,
        flops=2 * group * width * tokens * NY,
    )(zl[None], got, mine, swap(theirs, "core"), outer_momentum)
    partial = lax.all_to_all(partial, "x", 0, 0, tiled=True)
    group_weight = ring4(pair_weight, "x")

    own, gain_own, send, step = call(
        dwsum_body,
        (
            shape((part, width), f32),
            shape((part, 128), f32),
            shape((part, width + 128), bf16),
            half_short,
        ),
        4,
        scalars=1,
    )(zh[None], partial, pair_weight, step, partner(step, 4))
    keys_sent = shape((tokens, width), bf16)
    own_keys, up, down, over, step = call(
        keys_body,
        (shape((tokens, width), f32), keys_sent, keys_sent, keys_sent, half),
        7,
        scalars=2,
        after=1,
        flops=2 * group * width * tokens * NY,
    )(x[None], y[None], own, got, *group_weight, step, partner(step, 2))

    moments = shape((part, width), f32)
    new_w, new_wf, new_ws, tiles = call(
        update_body,
        (shape((part, width), bf16), moments, moments, shape((NX * NY, 8, 128), f32)),
        6,
        after=1,
    )(own_keys, own, swap(send, "zh"), weight, weight_first[0], weight_second[0], gain_own)
    tiles = lax.all_to_all(tiles, ("x", "y"), 0, 0, tiled=True)
    keys = call(sum_body, keys_sent, 4)(
        own_keys, shift(up, "y", 1), shift(down, "y", -1), shift(over, "y", 2)
    )
    outer_half, new_momentum = call(
        step_body, (half, shape(outer_momentum.shape, f32)), 4, scalars=1
    )(zl[None], step, partner(step, 1), outer_mine, packed)
    new_outer = call(join_body, shape(outer_params.shape, f32), 2, scalars=1)(
        core[None], outer_half, swap(outer_half, "core")
    )
    gain_grad = tiles[:, :ZH, :part].transpose(1, 0, 2).reshape(1, wide) / norm_gain
    new_g, new_gf, new_gs = adamw(norm_gain, gain_grad, gain_first, gain_second, rate_gain)
    return (
        keys[None],
        new_w[None],
        new_wf[None],
        new_ws[None],
        new_g,
        new_gf,
        new_gs,
        new_outer,
        new_momentum,
    )


def solution(mesh):
    grid = Mesh(mesh.devices.reshape(ZL, CORE, ZH, NX, NY), ISLAND + SHARD)
    block = P(ISLAND, SHARD, None)
    vector = P(ISLAND, None)
    fragment = P(SHARD, None)
    momentum = P(SHARD, ISLAND)
    return jax.shard_map(
        local,
        mesh=grid,
        in_specs=(block,) * 5 + (vector,) * 3 + (fragment, block, momentum),
        out_specs=(block,) * 4 + (vector,) * 3 + (fragment, momentum),
        check_vma=False,
    )
```

```python
import functools

import jax
import jax.numpy as jnp
from jax import lax
from jax.experimental import pallas as pl
from jax.experimental.pallas import tpu as pltpu
from jax.sharding import Mesh, PartitionSpec as P

beta_first = 0.9
beta_second = 0.95
adam_floor = 1e-08
weight_decay = 0.1
rate_weight = 0.02
rate_gain = 0.01
momentum_keep = 0.9
rate_outer = 0.7
norm_epsilon = 1e-06

bf16 = jnp.bfloat16
f32 = jnp.float32

ZL, CORE, ZH, NX, NY = 8, 2, 2, 4, 4
ISLAND = ("zl", "core")
SHARD = ("zh", "x", "y")
VMEM = pl.BlockSpec(memory_space=pltpu.VMEM)
ANY = pl.BlockSpec(memory_space=pl.ANY)
SMEM = pl.BlockSpec(memory_space=pltpu.SMEM)


def call(body, out_shape, n_in, *, scalars=0, after=0, flops=0, moved=1 << 20, vmem=40):
    return pl.pallas_call(
        body,
        out_shape=out_shape,
        in_specs=[SMEM] * scalars + [ANY] * after + [VMEM] * n_in,
        out_specs=jax.tree.map(lambda _: VMEM, out_shape),
        compiler_params=pltpu.CompilerParams(vmem_limit_bytes=vmem << 20),
        cost_estimate=pl.CostEstimate(flops=flops, bytes_accessed=moved, transcendentals=0),
    )


def adamw(param, grad, first, second, rate):
    first_new = beta_first * first + (1.0 - beta_first) * grad
    second_new = beta_second * second + (1.0 - beta_second) * grad * grad
    update = first_new / (jnp.sqrt(second_new) + adam_floor) + weight_decay * param
    return (param - rate * update, first_new, second_new)


def pack(tile, low):
    rows = tile.shape[0] // 2
    top, bottom = tile[:rows], tile[rows:]
    return (
        jnp.where(low, top, pltpu.roll(bottom, 64, 1)),
        jnp.where(low, pltpu.roll(top, 64, 1), bottom),
    )


def low_lanes(rows):
    return lax.broadcasted_iota(jnp.int32, (rows, 128), 1) < 64


def diff_body(core_ref, outer, island, mine, theirs, outer_mine):
    low = low_lanes(mine.shape[1])
    first = core_ref[0] == 0
    for pair in range(mine.shape[0]):
        cols = slice(128 * pair, 128 * pair + 128)
        whole = outer[:, cols]
        even, odd = pack(whole - island[:, cols].astype(f32), low)
        mine[pair] = jnp.where(first, even, odd)
        theirs[pair] = jnp.where(first, odd, even)
        even, odd = pack(whole, low)
        outer_mine[pair] = jnp.where(first, even, odd)


def halves_body(zh_ref, weight, weight_got, pair_weight):
    own, other = weight[...].astype(f32), weight_got[...].astype(f32)
    lower = zh_ref[0] == 0
    pair_weight[...] = jnp.concatenate(
        [jnp.where(lower, own, other), jnp.where(lower, other, own)], axis=0
    ).astype(bf16)


def norm_body(features, grads, gain, out):
    rows = features[...].astype(f32)
    scaled = rows * lax.rsqrt(jnp.mean(rows * rows, axis=1, keepdims=True) + norm_epsilon)
    turned = jnp.transpose(scaled * gain[...])
    width = turned.shape[0] // (ZH * NX * NY)
    turned_grads = jnp.transpose(grads[...].astype(f32)).astype(bf16)
    for y in range(NY):
        parts = []
        for x in range(NX):
            for zh in range(ZH):
                at = ((zh * NX + x) * NY + y) * width
                parts.append(turned[at : at + width])
        block = jnp.concatenate(parts, axis=0).astype(bf16)
        out[y, : block.shape[0], :] = block
        out[y, block.shape[0] :, :] = turned_grads


def dw_body(zl_ref, got, mine, theirs, moment, out, step, packed):
    part = out.shape[1]
    wide = NX * part
    grads = jnp.concatenate([got[s, wide:, :] for s in range(NY)], axis=1)
    for x in range(NX):
        rows = slice(x * part, (x + 1) * part)
        normed = jnp.concatenate([got[s, rows, :] for s in range(NY)], axis=1)
        out[x] = lax.dot_general(
            normed, grads, (((1,), (1,)), ((), ())), preferred_element_type=f32
        ).astype(bf16)
    half = packed.shape[0]
    packed[...] = jnp.concatenate([moment[:half], moment[half:]], axis=1)
    own = momentum_keep * momentum_keep * packed[...]
    for pair in range(step.shape[0]):
        drift = (mine[pair] + theirs[pair]) * ((1.0 + momentum_keep) / (ZL * CORE))
        step[pair] = jnp.where(zl_ref[0] == pair, drift + own, drift).astype(bf16)


def dwsum_body(zh_ref, got, weight, step, step_got, own, gain_own, send, step_out):
    half = own.shape[0]
    width = own.shape[1]
    low = zh_ref[0] == 0
    total = got[0].astype(f32)
    for s in range(1, NX):
        total = total + got[s].astype(f32)
    dots = jnp.sum(total * weight[...].astype(f32), axis=1, keepdims=True)
    own[...] = jnp.where(low, total[:half], total[half:])
    send[:, :width] = jnp.where(low, total[half:], total[:half]).astype(bf16)
    lane = lax.broadcasted_iota(jnp.int32, (half, 128), 1)
    first, second = dots[:half], dots[half:]
    first_hi, second_hi = first.astype(bf16).astype(f32), second.astype(bf16).astype(f32)
    first_lo = (first - first_hi).astype(bf16).astype(f32)
    second_lo = (second - second_hi).astype(bf16).astype(f32)
    packed = jnp.where(
        lane == 0,
        first_hi,
        jnp.where(lane == 1, second_hi, jnp.where(lane == 2, first_lo, second_lo)),
    )
    gain_own[...] = packed
    send[:, width:] = packed.astype(bf16)
    step_out[...] = (step[...].astype(f32) + step_got[...].astype(f32)).astype(bf16)


def keys_body(
    x_ref, y_ref, done, got, same, before, after, across, step, step_got, own, up, down, over, step_out
):
    del done
    part = same.shape[0]
    for to, out in ((0, own), (1, up), (NY - 1, down), (2, over)):
        s = lax.rem(y_ref[0] + to, NY)
        total = None
        for by, weight in ((0, same), (NX - 1, before), (1, after), (2, across)):
            source = lax.rem(x_ref[0] + by, NX)
            rows = got[s, pl.ds(pl.multiple_of(source * part, part), part), :]
            term = lax.dot_general(
                rows, weight[...], (((0,), (0,)), ((), ())), preferred_element_type=f32
            )
            total = term if total is None else total + term
        out[...] = total.astype(out.dtype)
    step_out[...] = step[...].astype(f32) + step_got[...].astype(f32)


def update_body(after, own, got, weight, first, second, gain_own, new_w, new_wf, new_ws, tiles):
    del after
    width = own.shape[1]
    grad = own[...] + got[:, :width].astype(f32)
    w, wf, ws = adamw(weight[...].astype(f32), grad, first[...], second[...], rate_weight)
    new_w[...] = w.astype(bf16)
    new_wf[...] = wf
    new_ws[...] = ws
    mine, theirs = gain_own[...], got[:, width:].astype(f32)
    total = (mine + pltpu.roll(mine, 126, 1)) + (theirs + pltpu.roll(theirs, 126, 1))
    total = jnp.concatenate([total, jnp.zeros((128 - total.shape[0], 128), f32)], axis=0)
    total = jnp.transpose(total)[:8]
    for at in range(tiles.shape[0]):
        tiles[at] = total


def step_body(zl_ref, step, step_got, outer_mine, packed, outer_out, moment_out):
    half = packed.shape[0]
    mine = jnp.zeros((half, 128), f32)
    for pair in range(outer_mine.shape[0]):
        both = step[pair] + step_got[pair]
        outer_out[pair] = outer_mine[pair] - rate_outer * both
        mine = jnp.where(zl_ref[0] == pair, both, mine)
    moment = packed[...]
    drift = (mine - momentum_keep * momentum_keep * moment) * (1.0 / (1.0 + momentum_keep))
    new = momentum_keep * moment + drift
    moment_out[:half] = new[:, :64]
    moment_out[half:] = new[:, 64:]


def sum_body(own, before, after, across, out):
    out[...] = (
        (own[...] + before[...].astype(f32)) + (after[...].astype(f32) + across[...].astype(f32))
    ).astype(bf16)


def join_body(core_ref, mine, got, out):
    rows = mine.shape[1]
    low = low_lanes(rows)
    first = core_ref[0] == 0
    for pair in range(mine.shape[0]):
        even = jnp.where(first, mine[pair], got[pair])
        odd = jnp.where(first, got[pair], mine[pair])
        cols = slice(128 * pair, 128 * pair + 128)
        out[:rows, cols] = jnp.where(low, even, pltpu.roll(odd, 64, 1))
        out[rows:, cols] = jnp.where(low, pltpu.roll(even, 64, 1), odd)


def swap(value, axis):
    return lax.ppermute(value, axis, [(0, 1), (1, 0)])


def shift(value, axis, by, size=4):
    return lax.ppermute(value, axis, [(i, (i + by) % size) for i in range(size)])


def ring4(value, axis):
    return value, shift(value, axis, 1), shift(value, axis, -1), shift(value, axis, 2)


def partner(value, by):
    return lax.ppermute(value, "zl", [(i, i ^ by) for i in range(ZL)])


def local(
    features,
    key_grads,
    key_weight,
    weight_first,
    weight_second,
    norm_gain,
    gain_first,
    gain_second,
    outer_params,
    island_params,
    outer_momentum,
):
    tokens, wide = features.shape[1:]
    width = key_weight.shape[2]
    part = wide // (ZH * NX * NY)
    group = wide // NY
    rows = outer_params.shape[0]
    zl, core = (lax.axis_index(a).astype(jnp.int32) for a in ISLAND)
    zh, x, y = (lax.axis_index(a).astype(jnp.int32) for a in SHARD)
    weight = key_weight[0]
    shape = jax.ShapeDtypeStruct
    half = shape((width // 128, rows // 2, 128), f32)
    half_short = shape(half.shape, bf16)

    sent = call(norm_body, shape((NY, group + width, tokens), bf16), 3, vmem=62)(
        features[0], key_grads[0], norm_gain
    )
    got = lax.all_to_all(sent, "y", 0, 0, tiled=True)
    pair_weight = call(
        halves_body, shape((ZH * part, width), bf16), 2, scalars=1, flops=int(1.3e10)
    )(
        zh[None], weight, swap(weight, "zh")
    )
    mine, theirs, outer_mine = call(diff_body, (half, half, half), 2, scalars=1)(
        core[None], outer_params, island_params[0]
    )
    partial, step, packed = call(
        dw_body,
        (shape((NX, ZH * part, width), bf16), half_short, shape(half.shape[1:], f32)),
        4,
        scalars=1,
        flops=2 * group * width * tokens * NY,
    )(zl[None], got, mine, swap(theirs, "core"), outer_momentum)
    partial = lax.all_to_all(partial, "x", 0, 0, tiled=True)
    group_weight = ring4(pair_weight, "x")

    own, gain_own, send, step = call(
        dwsum_body,
        (
            shape((part, width), f32),
            shape((part, 128), f32),
            shape((part, width + 128), bf16),
            half_short,
        ),
        4,
        scalars=1,
        vmem=62,
    )(zh[None], partial, pair_weight, step, partner(step, 4))
    keys_sent = shape((tokens, width), bf16)
    own_keys, up, down, over, step = call(
        keys_body,
        (shape((tokens, width), f32), keys_sent, keys_sent, keys_sent, half),
        7,
        scalars=2,
        after=1,
        vmem=62,
        flops=2 * group * width * tokens * NY,
    )(x[None], y[None], send, got, *group_weight, step, partner(step, 2))

    moments = shape((part, width), f32)
    new_w, new_wf, new_ws, tiles = call(
        update_body,
        (shape((part, width), bf16), moments, moments, shape((NX * NY, 8, 128), f32)),
        6,
        after=1,
    )(up, own, swap(send, "zh"), weight, weight_first[0], weight_second[0], gain_own)
    tiles = lax.all_to_all(tiles, ("x", "y"), 0, 0, tiled=True)
    keys = call(sum_body, keys_sent, 4)(
        own_keys, shift(up, "y", 1), shift(down, "y", -1), shift(over, "y", 2)
    )
    outer_half, new_momentum = call(
        step_body, (half, shape(outer_momentum.shape, f32)), 4, scalars=1
    )(zl[None], step, partner(step, 1), outer_mine, packed)
    new_outer = call(join_body, shape(outer_params.shape, f32), 2, scalars=1)(
        core[None], outer_half, swap(outer_half, "core")
    )
    gain_grad = tiles[:, :ZH, :part].transpose(1, 0, 2).reshape(1, wide) / norm_gain
    new_g, new_gf, new_gs = adamw(norm_gain, gain_grad, gain_first, gain_second, rate_gain)
    return (
        keys[None],
        new_w[None],
        new_wf[None],
        new_ws[None],
        new_g,
        new_gf,
        new_gs,
        new_outer,
        new_momentum,
    )


def solution(mesh):
    grid = Mesh(mesh.devices.reshape(ZL, CORE, ZH, NX, NY), ISLAND + SHARD)
    block = P(ISLAND, SHARD, None)
    vector = P(ISLAND, None)
    fragment = P(SHARD, None)
    momentum = P(SHARD, ISLAND)
    return jax.shard_map(
        local,
        mesh=grid,
        in_specs=(block,) * 5 + (vector,) * 3 + (fragment, block, momentum),
        out_specs=(block,) * 4 + (vector,) * 3 + (fragment, momentum),
        check_vma=False,
    )
```
